256 devices in a mesh: stn: 32 (over z_hi, y, core), tim: 8 (over x, z_lo).
Axes of the slice: x: 4, y: 4, z: 8 (z_hi: 4, z_lo: 2; z = z_hi * 2 + z_lo), core: 2. Of those that a mesh axis runs over, the one named last changes fastest.
Arguments:
- voltages: bfloat16 [2, 512, 524288], P(None, 'stn', 'tim'), may hold values from -6 to 6
- taps_weight: float32 [16, 1024], replicated, may hold values from -0.046875 to 0.046875
Outputs:
- visibilities: float32 [1024, 2, 512, 512], P(('stn', 'tim'))
The draws below stay inside these ranges and needn't reach their ends.
All inputs are finite; a program needn't handle non-finite values.
Results may differ from the reference program's by a relative error of at most 0.0047.
Values may be sent and summed in bfloat16 or wider, within the bound.
A program may use at most 192 MiB of HBM per device.

```python
import math
import jax
import jax.numpy as jnp
from jax import lax

K = 1024
TAPS = 16
NI = 512
SPEC = 512


def block_levels(stream_key, shape, cuts, smallest, largest):
    level = 1.0
    for position, parts in cuts:
        steps = jax.random.uniform(jax.random.fold_in(jax.random.fold_in(stream_key, 6), position), (parts,), jnp.float32, smallest / len(cuts), largest / len(cuts))
        level = level * jnp.repeat(jnp.exp(steps), shape[position] // parts).reshape((-1,) + (1,) * (len(shape) - 1 - position))
    return level


def normal_values(stream_key, extent, scale, most, shards=(), held_as=jnp.bfloat16):
    drawn = jax.random.normal(stream_key, extent, jnp.float32) * scale
    if len(shards) > 0:
        drawn = block_levels(stream_key, extent, shards, -0.22, 0.18) * drawn
    return jnp.clip(drawn, min=-most, max=most).astype(held_as)


def setup_inputs(seed: int = 0) -> dict:
    splits = jax.random.split(jax.random.key(seed), 3)
    voltages = normal_values(splits[0], (2, NI, SPEC * K), 1.0, 6.0, ((1, 32), (2, 8)))
    taps_weight = normal_values(splits[1], (TAPS, K), (K * TAPS) ** -0.5, 0.046875, (), jnp.float32)
    return dict(voltages=voltages, taps_weight=taps_weight)


def dft_table(size):
    index = jnp.arange(size, dtype=jnp.int32)
    phase = (index[:, None] * index[None, :]) % size
    angle = phase.astype(jnp.float32) * (2.0 * math.pi / size)
    cosine = jnp.cos(angle)
    sine = jnp.sin(angle)
    upper = jnp.stack([cosine, -sine], axis=1)
    lower = jnp.stack([sine, cosine], axis=1)
    return jnp.concatenate([upper, lower], axis=0).astype(jnp.bfloat16)


def reference(voltages, taps_weight):
    group = 32
    table = dft_table(K).astype(jnp.float32)
    blocks = voltages.reshape(2, NI // group, group, SPEC, K).transpose(1, 0, 2, 3, 4)

    def front(piece):
        padded = jnp.pad(piece, ((0, 0), (0, 0), (TAPS - 1, 0), (0, 0)))
        filtered = jnp.zeros((2, group, SPEC, K), jnp.float32)
        for tap in range(TAPS):
            start = TAPS - 1 - tap
            filtered = filtered + taps_weight[tap][None, None, None, :] * padded[:, :, start:start + SPEC, :].astype(jnp.float32)
        filtered = filtered.astype(jnp.bfloat16)
        stacked = filtered.transpose(1, 2, 0, 3).reshape(group * SPEC, 2 * K)
        spectra = jnp.einsum("rn,nqk->kqr", stacked.astype(jnp.float32), table)
        return spectra.astype(jnp.bfloat16).reshape(K, 2, group, SPEC)

    spectra = lax.map(front, blocks)
    spectra = spectra.transpose(1, 2, 0, 3, 4).reshape(K, 2, NI, SPEC)
    width = 8
    channels = spectra.reshape(K // width, width, 2, NI, SPEC)

    def correlate(piece):
        values = piece.astype(jnp.float32)
        real_part = jnp.einsum("cqip,cqjp->cij", values, values)
        cross = jnp.einsum("cip,cjp->cij", values[:, 1], values[:, 0])
        imag_part = cross - jnp.swapaxes(cross, 1, 2)
        return jnp.stack([real_part, imag_part], axis=1) / SPEC

    result = lax.map(correlate, channels)
    return result.reshape(K, 2, NI, NI)
```

```python
import math

import jax
import jax.numpy as jnp
from jax import lax
from jax.experimental import pallas as pl
from jax.experimental.pallas import tpu as pltpu
from jax.sharding import PartitionSpec as P

K = 1024
TAPS = 16


def shifted(shard, axis, by):
    length = lax.axis_size(axis)
    pairs = [(i, i + by) for i in range(length) if 0 <= i + by < length]
    return lax.ppermute(shard, axis, pairs)


def split_up(shard, dim, length):
    lengths = shard.shape
    parts = shard.reshape(*lengths[:dim], length, lengths[dim] // length, *lengths[dim + 1 :])
    return jnp.moveaxis(parts, dim, 0)


def joined_along(parts, dim):
    parts = jnp.moveaxis(parts, 0, dim)
    lengths = parts.shape
    return parts.reshape(*lengths[:dim], lengths[dim] * lengths[dim + 1], *lengths[dim + 2 :])


MESH = pl.DeviceIdType.MESH


def greet(ready, stations, pieces):
    stn, tim = lax.axis_index("stn"), lax.axis_index("tim")
    barrier = pltpu.get_barrier_semaphore()

    def column(i, _):
        pl.semaphore_signal(
            barrier, inc=1, device_id=((stn + i) % stations, tim), device_id_type=MESH
        )
        return 0

    lax.fori_loop(1, stations, column, 0)

    def row(i, _):
        pl.semaphore_signal(
            barrier, inc=1, device_id=(stn, (tim + i) % pieces), device_id_type=MESH
        )
        return 0

    lax.fori_loop(1, pieces, row, 0)
    pl.semaphore_wait(barrier, stations + pieces - 2)

    def passed(i, _):
        pl.semaphore_signal(
            ready, inc=1, device_id=(stn, (tim + i) % pieces), device_id_type=MESH
        )
        return 0

    lax.fori_loop(1, pieces, passed, 0)
    pl.semaphore_wait(ready, pieces - 1)


def exchange_kernel(stations, pieces, src, dst, ready, own_sem, send_sem, recv_sem):
    devices = stations * pieces
    me = lax.axis_index("stn") * pieces + lax.axis_index("tim")
    greet(ready, stations, pieces)
    own = pltpu.make_async_copy(src.at[me], dst.at[me], own_sem)
    own.start()

    def send(i, _):
        to = (me + (i * 77) % devices) % devices
        pltpu.make_async_remote_copy(
            src_ref=src.at[to],
            dst_ref=dst.at[me],
            send_sem=send_sem,
            recv_sem=recv_sem,
            device_id=(to // pieces, to % pieces),
            device_id_type=MESH,
        ).start()
        return 0

    lax.fori_loop(1, devices, send, 0)
    own.wait()
    others = src.at[pl.ds(0, devices - 1)]
    pltpu.make_async_copy(others, others, send_sem).wait()
    others = dst.at[pl.ds(0, devices - 1)]
    pltpu.make_async_copy(others, others, recv_sem).wait()


def exchanged(parts, stations, pieces):
    return pl.pallas_call(
        lambda *refs: exchange_kernel(stations, pieces, *refs),
        out_shape=jax.ShapeDtypeStruct(parts.shape, parts.dtype),
        in_specs=[pl.BlockSpec(memory_space=pl.ANY)],
        out_specs=pl.BlockSpec(memory_space=pl.ANY),
        scratch_shapes=[
            pltpu.SemaphoreType.REGULAR,
            pltpu.SemaphoreType.DMA,
            pltpu.SemaphoreType.DMA,
            pltpu.SemaphoreType.DMA,
        ],
        compiler_params=pltpu.CompilerParams(collective_id=0, has_side_effects=True),
    )(parts)


def joined_exchange(shard, axis, axes, splits, concats):
    sizes = [lax.axis_size(a) for a in axes]
    parts = split_up(shard, splits[0], sizes[0])
    parts = jnp.moveaxis(split_up(parts, splits[1] + 1, sizes[1]), 0, 1)
    inside = parts.shape[2:]
    parts = parts.reshape(-1, *inside)
    flat = parts.reshape(parts.shape[0], -1, 128)
    parts = exchanged(flat, *sizes)
    parts = joined_along(parts.reshape(*sizes, *inside), concats[0] + 1)
    return joined_along(parts, concats[1])


def dft_table(size):
    index = jnp.arange(size, dtype=jnp.int32)
    phase = index[:, None] * index[None, :] % size
    angle = phase.astype(jnp.float32) * (2.0 * math.pi / size)
    cosine = jnp.cos(angle)
    sine = jnp.sin(angle)
    upper = jnp.stack([cosine, -sine], axis=1)
    lower = jnp.stack([sine, cosine], axis=1)
    return jnp.concatenate([upper, lower], axis=0).astype(jnp.bfloat16)


def per_device(voltages, taps_weight):
    inputs_dev = voltages.shape[1]
    spec_dev = voltages.shape[2] // K
    blocks = voltages.reshape(2, inputs_dev, spec_dev, K)
    earlier = shifted(blocks[:, :, spec_dev - (TAPS - 1) :, :], "tim", 1)
    extended = jnp.concatenate([earlier, blocks], axis=2)
    filtered = jnp.zeros((2, inputs_dev, spec_dev, K), jnp.float32)
    for tap in range(TAPS):
        start = TAPS - 1 - tap
        filtered = filtered + taps_weight[tap][None, None, None, :] * extended[
            :, :, start : start + spec_dev, :
        ].astype(jnp.float32)
    filtered = filtered.astype(jnp.bfloat16)
    stacked = filtered.transpose(1, 2, 0, 3).reshape(inputs_dev * spec_dev, 2 * K)
    table = dft_table(K)
    spectra = jnp.einsum("rn,nqk->kqr", stacked, table, preferred_element_type=jnp.float32)
    columns = 2 * inputs_dev * spec_dev
    spectra = spectra.astype(jnp.bfloat16).reshape(K, columns)
    stations = lax.axis_size("stn")
    pieces = lax.axis_size("tim")
    ch_dev = K // (stations * pieces)
    turned = joined_exchange(spectra, ("stn", "tim"), ("stn", "tim"), (0, 0), (1, 1))
    layout = turned.reshape(ch_dev, pieces, stations, 2, inputs_dev, spec_dev).transpose(
        0, 3, 2, 4, 1, 5
    )
    total = pieces * spec_dev
    layout = layout.reshape(ch_dev, 2, stations * inputs_dev, total)
    real_part = jnp.einsum("cqip,cqjp->cij", layout, layout, preferred_element_type=jnp.float32)
    cross = jnp.einsum(
        "cip,cjp->cij", layout[:, 1], layout[:, 0], preferred_element_type=jnp.float32
    )
    imag_part = cross - jnp.swapaxes(cross, 1, 2)
    return jnp.stack([real_part, imag_part], axis=1) / total


def solution(mesh):
    return jax.shard_map(
        per_device,
        mesh=mesh,
        in_specs=(P(None, "stn", "tim"), P()),
        out_specs=P(("stn", "tim"), None, None, None),
        check_vma=False,
    )
```

```python
import math

import jax
import jax.numpy as jnp
import ml_dtypes
import numpy as np
from jax import lax
from jax.experimental import pallas as pl
from jax.experimental.pallas import tpu as pltpu
from jax.sharding import PartitionSpec as P

K = 1024
TAPS = 16
RADIX = 4
QUARTER = K // RADIX
LANES = 128
CHUNKS = K // LANES
A = 16
T = 64
TE = 16
MESH = pl.DeviceIdType.MESH
F32, BF16 = jnp.float32, jnp.bfloat16


def tables():
    k = np.arange(QUARTER)[None, :, None] * RADIX + np.arange(RADIX)[:, None, None]
    phase = (k * np.arange(QUARTER)[None, None, :]) % K
    angle = phase.astype(np.float64) * (2.0 * math.pi / K)
    both = np.concatenate([np.cos(angle), np.sin(angle)], axis=2)
    return both.astype(np.float32).astype(ml_dtypes.bfloat16)


def greet_start(stations, pieces):
    stn, tim = lax.axis_index("stn"), lax.axis_index("tim")
    barrier = pltpu.get_barrier_semaphore()

    def column(i, _):
        pl.semaphore_signal(
            barrier, inc=1, device_id=((stn + i) % stations, tim), device_id_type=MESH
        )
        return 0

    lax.fori_loop(1, stations, column, 0)

    def row(i, _):
        pl.semaphore_signal(
            barrier, inc=1, device_id=(stn, (tim + i) % pieces), device_id_type=MESH
        )
        return 0

    lax.fori_loop(1, pieces, row, 0)


def greet_pass(ready, stations, pieces):
    stn, tim = lax.axis_index("stn"), lax.axis_index("tim")
    pl.semaphore_wait(pltpu.get_barrier_semaphore(), stations + pieces - 2)

    def passed(i, _):
        pl.semaphore_signal(
            ready, inc=1, device_id=(stn, (tim + i) % pieces), device_id_type=MESH
        )
        return 0

    lax.fori_loop(1, pieces, passed, 0)


def fir_outputs(load, weights, times, low, high):
    blocks = {}
    outs = []
    for t in times:
        total = None
        for p in range(TAPS):
            b = t - p
            if b < low or b >= high:
                continue
            if b not in blocks:
                blocks[b] = load(b)
            term = weights[p] * blocks[b]
            total = term if total is None else total + term
        outs.append(total)
    return outs


def filter_block(x, w, stage, length, q, c, first, start_time, low, high, count):
    lanes = pl.multiple_of(c * LANES, LANES)
    weights = [
        jnp.broadcast_to(w[pl.ds(p, 1), pl.ds(lanes, LANES)], (A, LANES)) for p in range(TAPS)
    ]

    def load(b):
        at = pl.multiple_of((first + b) * K + lanes, LANES)
        return x[q, :, pl.ds(at, LANES)].astype(F32)

    outs = fir_outputs(load, weights, range(start_time, start_time + count), low, high)
    base = (q * CHUNKS + c) * A * length
    for i, out in enumerate(outs):
        yield base, i, out


def butterfly(stage, rows, h, length):
    v = []
    for q in range(2):
        for j in range(RADIX):
            base = (q * CHUNKS + 2 * j + h) * A * length
            v.append(stage[pl.ds(base + rows, length), :])
    re, im = v[:4], v[4:]
    a0r, a0i = re[0] + re[2], im[0] + im[2]
    a1r, a1i = re[0] - re[2], im[0] - im[2]
    b0r, b0i = re[1] + re[3], im[1] + im[3]
    b1r, b1i = re[1] - re[3], im[1] - im[3]
    return [
        (a0r + b0r, a0i + b0i),
        (a1r + b1i, a1i - b1r),
        (a0r - b0r, a0i - b0i),
        (a1r - b1i, a1i + b1r),
    ]


def dft(table, rows):
    return lax.dot_general(
        table, rows, (((1,), (1,)), ((), ())), preferred_element_type=F32
    )


def front_kernel(
    stations,
    pieces,
    x_hbm,
    w,
    table,
    main_out,
    extra_out,
    x,
    stage,
    stage_e,
    mixed,
    mixed_e,
    turned,
    halves,
    packed,
    ready,
    load_sem,
    own_sem,
    send_sem,
    recv_sem,
):
    devices = stations * pieces
    stn, tim = lax.axis_index("stn"), lax.axis_index("tim")
    me = stn * pieces + tim
    tail = (T - TAPS + 1) * K
    copies = []
    for i, (at, size) in enumerate(((tail, T * K - tail), (0, tail))):
        copy = pltpu.make_async_copy(
            x_hbm.at[:, :, pl.ds(at, size)], x.at[:, :, pl.ds(at, size)], load_sem.at[i]
        )
        copy.start()
        copies.append(copy)
    greet_start(stations, pieces)
    copies[0].wait()

    def fir_extra(i, _):
        q, c = i // CHUNKS, i % CHUNKS
        for base, t, out in filter_block(
            x, w, stage_e, TE, q, c, T - TAPS + 1, TAPS - 1, 0, TAPS - 1, TE - 1
        ):
            stage_e[pl.ds(base + t, A, stride=TE), :] = out
        stage_e[pl.ds((q * CHUNKS + c) * A * TE + TE - 1, A, stride=TE), :] = jnp.zeros(
            (A, LANES), F32
        )
        return 0

    lax.fori_loop(0, 2 * CHUNKS, fir_extra, 0)
    greet_pass(ready, stations, pieces)

    def mix_extra(a, _):
        group = (a // 4) * 128 + (a % 4) * TE
        for h in range(2):
            for r, (re, im) in enumerate(butterfly(stage_e, a * TE, h, TE)):
                top = pl.ds(pl.multiple_of(group, TE), TE)
                low = pl.ds(pl.multiple_of(group + 64, TE), TE)
                near = pl.ds(h * LANES, LANES)
                far = pl.ds(QUARTER + h * LANES, LANES)
                mixed_e[r, top, near] = re.astype(BF16)
                mixed_e[r, top, far] = im.astype(BF16)
                mixed_e[r, low, near] = im.astype(BF16)
                mixed_e[r, low, far] = (-re).astype(BF16)
        return 0

    lax.fori_loop(0, A, mix_extra, 0)
    lane = lax.broadcasted_iota(jnp.int32, (QUARTER, LANES), 1)
    slot = (lane % 64) // TE
    for r in range(RADIX):
        halves[r] = dft(table[r], mixed_e[r])

    def turn_extra(high, _):
        at = pl.multiple_of(high * LANES, LANES)
        parts = [halves[r, :, pl.ds(at, LANES)] for r in range(RADIX)]
        for low in range(4):
            out = None
            for r in range(RADIX):
                moved = parts[r]
                if r != low:
                    moved = pltpu.roll(moved, (TE * (r - low)) % LANES, 1)
                out = moved if out is None else jnp.where(slot == r, moved, out)
            turned[pl.ds(high * 4 + low, QUARTER, stride=A), :] = out
        return 0

    lax.fori_loop(0, 4, turn_extra, 0)

    def pack(into):
        def some(i, _):
            rows = turned[pl.ds(pl.multiple_of(i * 512, 512), 512), :]
            packed[into, pl.ds(pl.multiple_of(i * 32, 32), 32)] = rows.astype(BF16).reshape(
                32, A, LANES
            )
            return 0

        lax.fori_loop(0, QUARTER * A // 512, some, 0)

    def send_all(into, dst):
        def send(i, _):
            to = (me + (i * 77) % devices) % devices
            pltpu.make_async_remote_copy(
                src_ref=packed.at[into, to],
                dst_ref=dst.at[me],
                send_sem=send_sem.at[into],
                recv_sem=recv_sem.at[into],
                device_id=(to // pieces, to % pieces),
                device_id_type=MESH,
            ).start()
            return 0

        lax.fori_loop(1, devices, send, 0)

    pack(RADIX)
    pl.semaphore_wait(ready, pieces - 1)
    own_copies = [
        pltpu.make_async_copy(
            packed.at[i, me],
            (extra_out if i == RADIX else main_out.at[i]).at[me],
            own_sem.at[i],
        )
        for i in range(RADIX + 1)
    ]
    own_copies[RADIX].start()

    @pl.when(tim < pieces - 1)
    def _():
        send_all(RADIX, extra_out)

    copies[1].wait()

    def fir_main(i, _):
        q, c = i // CHUNKS, i % CHUNKS
        for base, t, out in filter_block(x, w, stage, T, q, c, 0, 0, 0, T, TAPS):
            stage[pl.ds(base + t, A, stride=T), :] = out

        def later(block, _):
            first = block * TAPS
            for base, t, out in filter_block(
                x, w, stage, T, q, c, first, 0, -TAPS, TAPS, TAPS
            ):
                stage[pl.ds(base + first + t, A, stride=T), :] = out
            return 0

        lax.fori_loop(1, T // TAPS, later, 0)
        return 0

    lax.fori_loop(0, 2 * CHUNKS, fir_main, 0)

    def mix_main(a, _):
        for h in range(2):
            for r, (re, im) in enumerate(butterfly(stage, a * T, h, T)):
                top = pl.ds(pl.multiple_of(a * 2 * T, T), T)
                low = pl.ds(pl.multiple_of(a * 2 * T + T, T), T)
                near = pl.ds(h * LANES, LANES)
                far = pl.ds(QUARTER + h * LANES, LANES)
                mixed[r, top, near] = re.astype(BF16)
                mixed[r, top, far] = im.astype(BF16)
                mixed[r, low, near] = im.astype(BF16)
                mixed[r, low, far] = (-re).astype(BF16)
        return 0

    lax.fori_loop(0, A, mix_main, 0)
    for r in range(RADIX):

        def transform(pair, _, r=r):
            rows = mixed[r, pl.ds(pl.multiple_of(pair * 256, 256), 256), :]
            out = dft(table[r], rows)
            for i in range(2):
                turned[pl.ds(pair * 2 + i, QUARTER, stride=A), :] = out[
                    :, i * LANES : (i + 1) * LANES
                ]
            return 0

        lax.fori_loop(0, A // 2, transform, 0)
        pack(r)
        own_copies[r].start()
        send_all(r, main_out.at[r])

    for copy in own_copies:
        copy.wait()
    for r in range(RADIX):
        others = packed.at[r, pl.ds(0, devices - 1)]
        pltpu.make_async_copy(others, others, send_sem.at[r]).wait()
        others = main_out.at[r, pl.ds(0, devices - 1)]
        pltpu.make_async_copy(others, others, recv_sem.at[r]).wait()
    senders = stations * (pieces - 1)

    @pl.when(tim < pieces - 1)
    def _():
        others = packed.at[RADIX, pl.ds(0, devices - 1)]
        pltpu.make_async_copy(others, others, send_sem.at[RADIX]).wait()
        others = extra_out.at[pl.ds(0, senders - 1)]
        pltpu.make_async_copy(others, others, recv_sem.at[RADIX]).wait()

    @pl.when(tim == pieces - 1)
    def _():
        others = extra_out.at[pl.ds(0, senders)]
        pltpu.make_async_copy(others, others, recv_sem.at[RADIX]).wait()


def correlate_kernel(main, extra, out, values, crossed):
    r = pl.program_id(0)
    pieces = main.shape[2]
    inputs = values.shape[0]
    lane = lax.broadcasted_iota(jnp.int32, (inputs, LANES), 1)
    for s in range(pieces):
        v = main[0, :, s].reshape(inputs, LANES)
        if s > 0:
            more = extra[:, s - 1].reshape(inputs, LANES).astype(F32)
            more = pltpu.roll(more, (LANES - TE * r) % LANES, 1)
            v = (v.astype(F32) + jnp.where(lane % 64 < TE, more, 0.0)).astype(BF16)
        at = pl.ds(s * LANES, LANES)
        values[:, at] = v
        turned = pltpu.roll(v.astype(F32), 64, 1)
        crossed[:, at] = jnp.where(lane < 64, -turned, turned).astype(BF16)
    scale = 1.0 / (pieces * T)
    out[0, 0] = dft(values[...], values[...]) * scale
    out[0, 1] = dft(values[...], crossed[...]) * scale


def per_device(voltages, taps_weight):
    stations, pieces = lax.axis_size("stn"), lax.axis_size("tim")
    devices = stations * pieces
    any_space = pl.BlockSpec(memory_space=pl.ANY)
    vmem = pl.BlockSpec(memory_space=pltpu.VMEM)
    main, extra = pl.pallas_call(
        lambda *refs: front_kernel(stations, pieces, *refs),
        out_shape=[
            jax.ShapeDtypeStruct((RADIX, devices, A, LANES), BF16),
            jax.ShapeDtypeStruct((devices, A, LANES), BF16),
        ],
        in_specs=[any_space, vmem, vmem],
        out_specs=[any_space, any_space],
        scratch_shapes=[
            pltpu.VMEM((2, A, T * K), BF16),
            pltpu.VMEM((2 * CHUNKS * A * T, LANES), F32),
            pltpu.VMEM((2 * CHUNKS * A * TE, LANES), F32),
            pltpu.VMEM((RADIX, A * 2 * T, 2 * QUARTER), BF16),
            pltpu.VMEM((RADIX, A * 2 * TE, 2 * QUARTER), BF16),
            pltpu.VMEM((QUARTER * A, LANES), F32),
            pltpu.VMEM((RADIX, QUARTER, A * 2 * TE), F32),
            pltpu.VMEM((RADIX + 1, devices, A, LANES), BF16),
            pltpu.SemaphoreType.REGULAR,
            pltpu.SemaphoreType.DMA((2,)),
            pltpu.SemaphoreType.DMA((RADIX + 1,)),
            pltpu.SemaphoreType.DMA((RADIX + 1,)),
            pltpu.SemaphoreType.DMA((RADIX + 1,)),
        ],
        compiler_params=pltpu.CompilerParams(
            collective_id=0, has_side_effects=True, vmem_limit_bytes=56 << 20
        ),
    )(voltages, taps_weight, jnp.asarray(tables()))
    inputs = stations * A
    return pl.pallas_call(
        correlate_kernel,
        grid=(RADIX,),
        out_shape=jax.ShapeDtypeStruct((RADIX, 2, inputs, inputs), F32),
        in_specs=[
            pl.BlockSpec((1, stations, pieces, A, LANES), lambda r: (r, 0, 0, 0, 0)),
            pl.BlockSpec((stations, pieces, A, LANES), lambda r: (0, 0, 0, 0)),
        ],
        out_specs=pl.BlockSpec((1, 2, inputs, inputs), lambda r: (r, 0, 0, 0)),
        scratch_shapes=[
            pltpu.VMEM((inputs, pieces * LANES), BF16),
            pltpu.VMEM((inputs, pieces * LANES), BF16),
        ],
        compiler_params=pltpu.CompilerParams(vmem_limit_bytes=40 << 20),
    )(
        main.reshape(RADIX, stations, pieces, A, LANES),
        extra.reshape(stations, pieces, A, LANES),
    )


def solution(mesh):
    return jax.shard_map(
        per_device,
        mesh=mesh,
        in_specs=(P(None, "stn", "tim"), P()),
        out_specs=P(("stn", "tim"), None, None, None),
        check_vma=False,
    )
```

```python
import math

import jax
import jax.numpy as jnp
import ml_dtypes
import numpy as np
from jax import lax
from jax.experimental import pallas as pl
from jax.experimental.pallas import tpu as pltpu
from jax.sharding import PartitionSpec as P

K = 1024
TAPS = 16
RADIX = 4
QUARTER = K // RADIX
LANES = 128
CHUNKS = K // LANES
A = 16
T = 64
TE = 16
GROUPS = T // TE
PLANES = 8
PLANE = 32
SIDE = PLANES // 2
MESH = pl.DeviceIdType.MESH
F32, BF16 = jnp.float32, jnp.bfloat16


def place(u, pieces):
    z, w = u // PLANE, u % PLANE
    return (z // 2) * 8 + w // 4, (w % 4) * 2 + z % 2


def tables():
    stn, tim = place(np.arange(QUARTER), 8)
    k = (stn * 8 + tim)[None, :, None] * RADIX + np.arange(RADIX)[:, None, None]
    phase = (k * np.arange(QUARTER)[None, None, :]) % K
    angle = phase.astype(np.float64) * (2.0 * math.pi / K)
    both = np.concatenate([np.cos(angle), np.sin(angle)], axis=2)
    return both.astype(np.float32).astype(ml_dtypes.bfloat16)


def greet_start(stations, pieces):
    stn, tim = lax.axis_index("stn"), lax.axis_index("tim")
    barrier = pltpu.get_barrier_semaphore()

    def column(i, _):
        pl.semaphore_signal(
            barrier, inc=1, device_id=((stn + i) % stations, tim), device_id_type=MESH
        )
        return 0

    lax.fori_loop(1, stations, column, 0)

    def row(i, _):
        pl.semaphore_signal(
            barrier, inc=1, device_id=(stn, (tim + i) % pieces), device_id_type=MESH
        )
        return 0

    lax.fori_loop(1, pieces, row, 0)


def greet_pass(ready, stations, pieces):
    stn, tim = lax.axis_index("stn"), lax.axis_index("tim")
    pl.semaphore_wait(pltpu.get_barrier_semaphore(), stations + pieces - 2)

    def passed(i, _):
        pl.semaphore_signal(
            ready, inc=1, device_id=(stn, (tim + i) % pieces), device_id_type=MESH
        )
        return 0

    lax.fori_loop(1, pieces, passed, 0)


def fir_outputs(load, weights, times, low, high):
    blocks = {}
    outs = []
    for t in times:
        total = None
        for p in range(TAPS):
            b = t - p
            if b < low or b >= high:
                continue
            if b not in blocks:
                blocks[b] = load(b)
            term = weights[p] * blocks[b]
            total = term if total is None else total + term
        outs.append(total)
    return outs


def filter_group(x, w, stage, first, start_time, low, high, count):
    def one(i, _):
        q, c = i // CHUNKS, i % CHUNKS
        lanes = pl.multiple_of(c * LANES, LANES)
        weights = [
            jnp.broadcast_to(w[pl.ds(p, 1), pl.ds(lanes, LANES)], (A, LANES))
            for p in range(TAPS)
        ]

        def load(b):
            at = pl.multiple_of((first + b) * K + lanes, LANES)
            return x[q, :, pl.ds(at, LANES)].astype(F32)

        outs = fir_outputs(load, weights, range(start_time, start_time + count), low, high)
        base = i * A * TE
        for t, out in enumerate(outs):
            stage[pl.ds(base + t, A, stride=TE), :] = out
        if count < TE:
            stage[pl.ds(base + count, A, stride=TE), :] = jnp.zeros((A, LANES), F32)
        return 0

    lax.fori_loop(0, 2 * CHUNKS, one, 0)


def butterfly(stage, rows, h, length):
    v = []
    for q in range(2):
        for j in range(RADIX):
            base = (q * CHUNKS + 2 * j + h) * A * length
            v.append(stage[pl.ds(base + rows, length), :])
    re, im = v[:4], v[4:]
    a0r, a0i = re[0] + re[2], im[0] + im[2]
    a1r, a1i = re[0] - re[2], im[0] - im[2]
    b0r, b0i = re[1] + re[3], im[1] + im[3]
    b1r, b1i = re[1] - re[3], im[1] - im[3]
    return [
        (a0r + b0r, a0i + b0i),
        (a1r + b1i, a1i - b1r),
        (a0r - b0r, a0i - b0i),
        (a1r - b1i, a1i + b1r),
    ]


def dft(table, rows):
    return lax.dot_general(
        table, rows, (((1,), (1,)), ((), ())), preferred_element_type=F32
    )


def transform_group(table, stage, mixed, halves, turned, packed, slot_to):
    def mix(a, _):
        group = (a // 4) * 128 + (a % 4) * TE
        for h in range(2):
            for r, (re, im) in enumerate(butterfly(stage, a * TE, h, TE)):
                top = pl.ds(pl.multiple_of(group, TE), TE)
                low = pl.ds(pl.multiple_of(group + 64, TE), TE)
                near = pl.ds(h * LANES, LANES)
                far = pl.ds(QUARTER + h * LANES, LANES)
                mixed[r, top, near] = re.astype(BF16)
                mixed[r, top, far] = im.astype(BF16)
                mixed[r, low, near] = im.astype(BF16)
                mixed[r, low, far] = (-re).astype(BF16)
        return 0

    lax.fori_loop(0, A, mix, 0)
    slot = (lax.broadcasted_iota(jnp.int32, (QUARTER, LANES), 1) % 64) // TE
    for r in range(RADIX):
        halves[r] = dft(table[r], mixed[r])

    def turn(high, _):
        at = pl.multiple_of(high * LANES, LANES)
        parts = [halves[r, :, pl.ds(at, LANES)] for r in range(RADIX)]
        for low in range(4):
            turned[pl.ds(high * 4 + low, QUARTER, stride=A), :] = regroup(parts, low, slot)
        return 0

    lax.fori_loop(0, 4, turn, 0)

    def pack(i, _):
        rows = turned[pl.ds(pl.multiple_of(i * 512, 512), 512), :]
        packed[slot_to, pl.ds(pl.multiple_of(i * 32, 32), 32)] = rows.astype(BF16).reshape(
            32, A, LANES
        )
        return 0

    lax.fori_loop(0, QUARTER * A // 512, pack, 0)


def regroup(parts, low, slot):
    out = None
    for i, part in enumerate(parts):
        moved = part
        if i != low:
            moved = pltpu.roll(part, (TE * (i - low)) % LANES, 1)
        out = moved if out is None else jnp.where(slot == i, moved, out)
    return out


def gather(tiles, values, crossed, r, start, stations):
    rows = stations * A
    at = pl.ds(pl.multiple_of(start * A, A), rows)
    lane = lax.broadcasted_iota(jnp.int32, (rows, LANES), 1)
    slot = (lane % 64) // TE
    for half in range(2):
        parts = [
            tiles[pl.ds(start, stations), half * 4 + i].reshape(rows, LANES).astype(F32)
            for i in range(4)
        ]
        out = regroup(parts, r, slot)
        other = pltpu.roll(out, 64, 1)
        lanes = pl.ds(half * LANES, LANES)
        values[r, at, lanes] = out.astype(BF16)
        crossed[r, at, lanes] = jnp.where(lane < 64, -other, other).astype(BF16)


def front_kernel(
    stations,
    pieces,
    x_hbm,
    w,
    table,
    power_out,
    border_out,
    x,
    stage,
    mixed,
    halves,
    turned,
    packed,
    heard,
    joined,
    landed,
    values,
    crossed,
    power,
    ready,
    load_sem,
    own_sem,
    send_sem,
    recv_sem,
    heard_send,
    heard_recv,
    border_send,
):
    devices = stations * pieces
    inputs = stations * A
    stn, tim = lax.axis_index("stn"), lax.axis_index("tim")
    z, w_me = (stn // 8) * 2 + tim % 2, (stn % 8) * 4 + tim // 2
    me = z * PLANE + w_me
    side = 2 * (z % 2) - 1
    front, back = GROUPS, 0
    copies = []
    for i in range(2):
        part = pl.ds(i * (T // 2) * K, (T // 2) * K)
        copy = pltpu.make_async_copy(x_hbm.at[:, :, part], x.at[:, :, part], load_sem.at[i])
        copy.start()
        copies.append(copy)
    greet_start(stations, pieces)
    copies[0].wait()

    def finish(slot_to):
        transform_group(table, stage, mixed, halves, turned, packed, slot_to)

    def own(g):
        return pltpu.make_async_copy(
            packed.at[g, me], landed.at[g - 1, stn, tim], own_sem.at[g - 1]
        )

    def send_group(g):
        own(g).start()

        def send(i, _):
            to = (me + (i * 77) % devices) % devices
            pltpu.make_async_remote_copy(
                src_ref=packed.at[g, to],
                dst_ref=landed.at[g - 1, stn, tim],
                send_sem=send_sem.at[g - 1],
                recv_sem=recv_sem.at[g - 1],
                device_id=place(to, pieces),
                device_id_type=MESH,
            ).start()
            return 0

        lax.fori_loop(1, devices, send, 0)

    def some(ref, count):
        return ref.at[0, pl.ds(0, count)]

    def wait_for(sem, count):
        tiles = some(packed, count)
        pltpu.make_async_copy(tiles, tiles, sem).wait()

    def ours(i):
        return (z + PLANES + side * i) % PLANES

    def theirs(i):
        return (z + PLANES - side * (1 + i)) % PLANES

    def tell(slot_from, step, to):
        for i in range(SIDE):
            pltpu.make_async_remote_copy(
                src_ref=packed.at[slot_from, pl.ds(theirs(i) * PLANE, PLANE)],
                dst_ref=heard.at[step, pl.ds(i * PLANE, PLANE)],
                send_sem=heard_send.at[step],
                recv_sem=heard_recv.at[step],
                device_id=(stn, to),
                device_id_type=MESH,
            ).start()

    def join(slot_from, step):
        def add(n, _):
            at = pl.multiple_of(ours(n // 4) * PLANE + (n % 4) * 8, 8)
            here = packed[slot_from, pl.ds(at, 8)].astype(F32)
            there = heard[step, pl.ds(n * 8, 8)].astype(F32)
            joined[step, pl.ds(n * 8, 8)] = (here + there).astype(BF16)
            return 0

        lax.fori_loop(0, SIDE * PLANE // 8, add, 0)

    def send_border(step, piece, sem):
        def send(n, _):
            i, j = n % SIDE, n // SIDE
            to = (w_me + j * 13) % PLANE
            pltpu.make_async_remote_copy(
                src_ref=joined.at[step, i * PLANE + to],
                dst_ref=border_out.at[stn, piece],
                send_sem=sem,
                recv_sem=recv_sem.at[GROUPS - 1],
                device_id=place(ours(i) * PLANE + to, pieces),
                device_id_type=MESH,
            ).start()
            return 0

        lax.fori_loop(1, SIDE * PLANE, send, 0)

    filter_group(x, w, stage, TE, 0, -TAPS, TE, TE)
    greet_pass(ready, stations, pieces)
    finish(1)
    pl.semaphore_wait(ready, pieces - 1)
    send_group(1)
    copies[1].wait()
    filter_group(x, w, stage, T - TAPS + 1, TAPS - 1, 0, TAPS - 1, TE - 1)
    finish(front)

    @pl.when(tim < pieces - 1)
    def _():
        tell(front, 0, tim + 1)

    filter_group(x, w, stage, 0, 0, 0, TE, TE)
    finish(back)

    @pl.when(tim > 0)
    def _():
        tell(back, 1, tim - 1)

    for g in (2, 3):
        filter_group(x, w, stage, g * TE, 0, -TAPS, TE, TE)
        finish(g)
        send_group(g)

    @pl.when(tim > 0)
    def _():
        wait_for(heard_recv.at[0], SIDE * PLANE)
        join(back, 0)
        pltpu.make_async_copy(
            joined.at[0, w_me], border_out.at[stn, tim], own_sem.at[GROUPS - 1]
        ).start()
        send_border(0, tim, border_send.at[0])

    @pl.when(tim == 0)
    def _():
        pltpu.make_async_copy(
            packed.at[back, me], border_out.at[stn, tim], own_sem.at[GROUPS - 1]
        ).start()

        def send(i, _):
            to = (me + (i * 77) % devices) % devices
            pltpu.make_async_remote_copy(
                src_ref=packed.at[back, to],
                dst_ref=border_out.at[stn, tim],
                send_sem=border_send.at[0],
                recv_sem=recv_sem.at[GROUPS - 1],
                device_id=place(to, pieces),
                device_id_type=MESH,
            ).start()
            return 0

        lax.fori_loop(1, devices, send, 0)

    @pl.when(tim < pieces - 1)
    def _():
        wait_for(heard_recv.at[1], SIDE * PLANE)
        join(front, 1)
        pltpu.make_async_copy(
            joined.at[1, w_me], border_out.at[stn, tim + 1], own_sem.at[GROUPS]
        ).start()
        send_border(1, tim + 1, border_send.at[1])

    for g in range(1, GROUPS):
        own(g).wait()
        wait_for(recv_sem.at[g - 1], devices - 1)
        for r in range(RADIX):

            def collect(n, _, g=g, r=r):
                gather(landed.at[g - 1], values, crossed, r, n * 8, 8)
                return 0

            lax.fori_loop(0, stations // 8, collect, 0)

            def multiply(i, _, g=g, r=r):
                rows = pl.ds(pl.multiple_of(i * 256, 256), 256)
                for q, other in enumerate((values, crossed)):
                    more = dft(values[r, rows, :], other[r])
                    if g > 1:
                        more = power[r, q, rows, :] + more
                    power[r, q, rows, :] = more
                return 0

            lax.fori_loop(0, inputs // 256, multiply, 0)
            if g == GROUPS - 1:
                pltpu.make_async_copy(power.at[r], power_out.at[r], load_sem.at[0]).start()
                pltpu.make_async_copy(power.at[r], power_out.at[r], load_sem.at[0]).wait()

    for g in range(1, GROUPS):
        wait_for(send_sem.at[g - 1], devices - 1)

    def own_border(i):
        pltpu.make_async_copy(packed.at[0, 0], packed.at[0, 1], own_sem.at[i]).wait()

    own_border(GROUPS - 1)

    @pl.when(tim == 0)
    def _():
        wait_for(border_send.at[0], devices - 1)

    @pl.when(tim > 0)
    def _():
        wait_for(heard_send.at[1], SIDE * PLANE)
        wait_for(border_send.at[0], SIDE * PLANE - 1)

    @pl.when(tim < pieces - 1)
    def _():
        wait_for(heard_send.at[0], SIDE * PLANE)
        wait_for(border_send.at[1], SIDE * PLANE - 1)
        own_border(GROUPS)
        wait_for(recv_sem.at[GROUPS - 1], devices - 2)

    @pl.when(tim == pieces - 1)
    def _():
        wait_for(recv_sem.at[GROUPS - 1], devices - 1)


def last_kernel(power, tiles, out, values, crossed):
    step = pl.program_id(0)
    pieces = tiles.shape[1]
    for r in range(RADIX):

        @pl.when(step == r)
        def _(r=r):
            gather(tiles, values, crossed, r, 0, tiles.shape[0])

            for q, other in enumerate((values, crossed)):
                more = dft(values[r], other[r])
                out[0, q] = (power[0, q] + more) * (1.0 / (pieces * T))


def per_device(voltages, taps_weight):
    stations, pieces = lax.axis_size("stn"), lax.axis_size("tim")
    devices = stations * pieces
    inputs = stations * A
    any_space = pl.BlockSpec(memory_space=pl.ANY)
    vmem = pl.BlockSpec(memory_space=pltpu.VMEM)
    lanes = pieces * 2 * TE
    power, border = pl.pallas_call(
        lambda *refs: front_kernel(stations, pieces, *refs),
        out_shape=[
            jax.ShapeDtypeStruct((RADIX, 2, inputs, inputs), F32),
            jax.ShapeDtypeStruct((stations, pieces, A, LANES), BF16),
        ],
        in_specs=[any_space, vmem, vmem],
        out_specs=[any_space] * 2,
        scratch_shapes=[
            pltpu.VMEM((2, A, T * K), BF16),
            pltpu.VMEM((2 * CHUNKS * A * TE, LANES), F32),
            pltpu.VMEM((RADIX, A * 2 * TE, 2 * QUARTER), BF16),
            pltpu.VMEM((RADIX, QUARTER, A * 2 * TE), F32),
            pltpu.VMEM((QUARTER * A, LANES), F32),
            pltpu.VMEM((GROUPS + 1, devices, A, LANES), BF16),
            pltpu.VMEM((2, SIDE * PLANE, A, LANES), BF16),
            pltpu.VMEM((2, SIDE * PLANE, A, LANES), BF16),
            pltpu.VMEM((GROUPS - 1, stations, pieces, A, LANES), BF16),
            pltpu.VMEM((RADIX, inputs, lanes), BF16),
            pltpu.VMEM((RADIX, inputs, lanes), BF16),
            pltpu.VMEM((RADIX, 2, inputs, inputs), F32),
            pltpu.SemaphoreType.REGULAR,
            pltpu.SemaphoreType.DMA((2,)),
            pltpu.SemaphoreType.DMA((GROUPS + 1,)),
            pltpu.SemaphoreType.DMA((GROUPS - 1,)),
            pltpu.SemaphoreType.DMA((GROUPS,)),
            pltpu.SemaphoreType.DMA((2,)),
            pltpu.SemaphoreType.DMA((2,)),
            pltpu.SemaphoreType.DMA((2,)),
        ],
        compiler_params=pltpu.CompilerParams(
            collective_id=0, has_side_effects=True, vmem_limit_bytes=56 << 20
        ),
    )(voltages, taps_weight, jnp.asarray(tables()))
    block = pl.BlockSpec((1, 2, inputs, inputs), lambda r: (r, 0, 0, 0))
    return pl.pallas_call(
        last_kernel,
        grid=(RADIX,),
        out_shape=jax.ShapeDtypeStruct((RADIX, 2, inputs, inputs), F32),
        in_specs=[
            block,
            pl.BlockSpec((stations, pieces, A, LANES), lambda r: (0, 0, 0, 0)),
        ],
        out_specs=block,
        scratch_shapes=[
            pltpu.VMEM((RADIX, inputs, lanes), BF16),
            pltpu.VMEM((RADIX, inputs, lanes), BF16),
        ],
        compiler_params=pltpu.CompilerParams(vmem_limit_bytes=60 << 20),
    )(power, border)


def solution(mesh):
    return jax.shard_map(
        per_device,
        mesh=mesh,
        in_specs=(P(None, "stn", "tim"), P()),
        out_specs=P(("stn", "tim"), None, None, None),
        check_vma=False,
    )
```

```python
import math

import jax
import jax.numpy as jnp
import ml_dtypes
import numpy as np
from jax import lax
from jax.experimental import pallas as pl
from jax.experimental.pallas import tpu as pltpu
from jax.sharding import PartitionSpec as P

K = 1024
TAPS = 16
RADIX = 4
QUARTER = K // RADIX
LANES = 128
CHUNKS = K // LANES
A = 16
T = 64
TE = 16
GROUPS = T // TE
PLANES = 8
PLANE = 32
SIDE = PLANES // 2
MESH = pl.DeviceIdType.MESH
F32, BF16 = jnp.float32, jnp.bfloat16


def place(u, pieces):
    z, w = u // PLANE, u % PLANE
    return (z // 2) * 8 + w // 4, (w % 4) * 2 + z % 2


def tables():
    stn, tim = place(np.arange(QUARTER), 8)
    k = (stn * 8 + tim)[None, :, None] * RADIX + np.arange(RADIX)[:, None, None]
    phase = (k * np.arange(QUARTER)[None, None, :]) % K
    angle = phase.astype(np.float64) * (2.0 * math.pi / K)
    both = np.concatenate([np.cos(angle), np.sin(angle)], axis=2)
    return both.astype(np.float32).astype(ml_dtypes.bfloat16)


def greet_start(stations, pieces):
    stn, tim = lax.axis_index("stn"), lax.axis_index("tim")
    barrier = pltpu.get_barrier_semaphore()

    def column(i, _):
        pl.semaphore_signal(
            barrier, inc=1, device_id=((stn + i) % stations, tim), device_id_type=MESH
        )
        return 0

    lax.fori_loop(1, stations, column, 0)

    def row(i, _):
        pl.semaphore_signal(
            barrier, inc=1, device_id=(stn, (tim + i) % pieces), device_id_type=MESH
        )
        return 0

    lax.fori_loop(1, pieces, row, 0)


def greet_pass(ready, stations, pieces):
    stn, tim = lax.axis_index("stn"), lax.axis_index("tim")
    pl.semaphore_wait(pltpu.get_barrier_semaphore(), stations + pieces - 2)

    def passed(i, _):
        pl.semaphore_signal(
            ready, inc=1, device_id=(stn, (tim + i) % pieces), device_id_type=MESH
        )
        return 0

    lax.fori_loop(1, pieces, passed, 0)


def fir_outputs(load, weights, times, low, high):
    blocks = {}
    outs = []
    for t in times:
        total = None
        for p in range(TAPS):
            b = t - p
            if b < low or b >= high:
                continue
            if b not in blocks:
                blocks[b] = load(b)
            term = weights[p] * blocks[b]
            total = term if total is None else total + term
        outs.append(total)
    return outs


def filter_group(x, w, stage, first, start_time, low, high, count):
    def one(i, _):
        q, c = i // CHUNKS, i % CHUNKS
        lanes = pl.multiple_of(c * LANES, LANES)
        weights = [
            jnp.broadcast_to(w[pl.ds(p, 1), pl.ds(lanes, LANES)], (A, LANES))
            for p in range(TAPS)
        ]

        def load(b):
            at = pl.multiple_of((first + b) * K + lanes, LANES)
            return x[q, :, pl.ds(at, LANES)].astype(F32)

        outs = fir_outputs(load, weights, range(start_time, start_time + count), low, high)
        base = i * A * TE
        for t, out in enumerate(outs):
            stage[pl.ds(base + t, A, stride=TE), :] = out
        if count < TE:
            stage[pl.ds(base + count, A, stride=TE), :] = jnp.zeros((A, LANES), F32)
        return 0

    lax.fori_loop(0, 2 * CHUNKS, one, 0)


def butterfly(stage, rows, h, length):
    v = []
    for q in range(2):
        for j in range(RADIX):
            base = (q * CHUNKS + 2 * j + h) * A * length
            v.append(stage[pl.ds(base + rows, length), :])
    re, im = v[:4], v[4:]
    a0r, a0i = re[0] + re[2], im[0] + im[2]
    a1r, a1i = re[0] - re[2], im[0] - im[2]
    b0r, b0i = re[1] + re[3], im[1] + im[3]
    b1r, b1i = re[1] - re[3], im[1] - im[3]
    return [
        (a0r + b0r, a0i + b0i),
        (a1r + b1i, a1i - b1r),
        (a0r - b0r, a0i - b0i),
        (a1r - b1i, a1i + b1r),
    ]


def dft(table, rows):
    return lax.dot_general(
        table, rows, (((1,), (1,)), ((), ())), preferred_element_type=F32
    )


def transform_group(table, stage, mixed, halves, turned, packed, slot_to):
    def mix(a, _):
        group = (a // 4) * 128 + (a % 4) * TE
        for h in range(2):
            for r, (re, im) in enumerate(butterfly(stage, a * TE, h, TE)):
                top = pl.ds(pl.multiple_of(group, TE), TE)
                low = pl.ds(pl.multiple_of(group + 64, TE), TE)
                near = pl.ds(h * LANES, LANES)
                far = pl.ds(QUARTER + h * LANES, LANES)
                mixed[r, top, near] = re.astype(BF16)
                mixed[r, top, far] = im.astype(BF16)
                mixed[r, low, near] = im.astype(BF16)
                mixed[r, low, far] = (-re).astype(BF16)
        return 0

    lax.fori_loop(0, A, mix, 0)
    slot = (lax.broadcasted_iota(jnp.int32, (QUARTER, LANES), 1) % 64) // TE
    for r in range(RADIX):
        halves[r] = dft(table[r], mixed[r])

    def turn(high, _):
        at = pl.multiple_of(high * LANES, LANES)
        parts = [halves[r, :, pl.ds(at, LANES)] for r in range(RADIX)]
        for low in range(4):
            turned[pl.ds(high * 4 + low, QUARTER, stride=A), :] = regroup(parts, low, slot)
        return 0

    lax.fori_loop(0, 4, turn, 0)

    def pack(i, _):
        rows = turned[pl.ds(pl.multiple_of(i * 512, 512), 512), :]
        packed[slot_to, pl.ds(pl.multiple_of(i * 32, 32), 32)] = rows.astype(BF16).reshape(
            32, A, LANES
        )
        return 0

    lax.fori_loop(0, QUARTER * A // 512, pack, 0)


def regroup(parts, low, slot):
    out = None
    for i, part in enumerate(parts):
        moved = part
        if i != low:
            moved = pltpu.roll(part, (TE * (i - low)) % LANES, 1)
        out = moved if out is None else jnp.where(slot == i, moved, out)
    return out


def gather(tiles, values, crossed, r, start, stations):
    rows = stations * A
    at = pl.ds(pl.multiple_of(start * A, A), rows)
    lane = lax.broadcasted_iota(jnp.int32, (rows, LANES), 1)
    slot = (lane % 64) // TE
    for half in range(2):
        parts = [
            tiles[pl.ds(start, stations), half * 4 + i].reshape(rows, LANES).astype(F32)
            for i in range(4)
        ]
        out = regroup(parts, r, slot)
        other = pltpu.roll(out, 64, 1)
        lanes = pl.ds(half * LANES, LANES)
        values[r, at, lanes] = out.astype(BF16)
        crossed[r, at, lanes] = jnp.where(lane < 64, -other, other).astype(BF16)


def front_kernel(
    stations,
    pieces,
    x_hbm,
    w,
    table,
    power_out,
    border_out,
    x,
    stage,
    mixed,
    halves,
    turned,
    packed,
    heard,
    joined,
    landed,
    values,
    crossed,
    power,
    ready,
    load_sem,
    own_sem,
    send_sem,
    recv_sem,
    heard_send,
    heard_recv,
    border_send,
):
    devices = stations * pieces
    inputs = stations * A
    stn, tim = lax.axis_index("stn"), lax.axis_index("tim")
    z, w_me = (stn // 8) * 2 + tim % 2, (stn % 8) * 4 + tim // 2
    me = z * PLANE + w_me
    side = 2 * (z % 2) - 1
    front, back = GROUPS, 0
    copies = []
    for i in range(2):
        part = pl.ds(i * (T // 2) * K, (T // 2) * K)
        copy = pltpu.make_async_copy(x_hbm.at[:, :, part], x.at[:, :, part], load_sem.at[i])
        copy.start()
        copies.append(copy)
    greet_start(stations, pieces)
    copies[0].wait()

    def finish(slot_to):
        transform_group(table, stage, mixed, halves, turned, packed, slot_to)

    def own(g):
        return pltpu.make_async_copy(
            packed.at[g, me], landed.at[g - 1, stn, tim], own_sem.at[g - 1]
        )

    def send_planes(copy, planes):
        levels = [(i, p * PLANE, lax.div(p, 2) * 8, lax.rem(p, 2)) for i, p in planes]

        def sends(j, levels):
            to = lax.rem(w_me + j * 13, PLANE)
            row, column = lax.div(to, 4), lax.rem(to, 4) * 2
            for i, start, stn_base, tim_base in levels:
                copy(i, start + to, (stn_base + row, tim_base + column)).start()

        sends(0, levels[1:])

        def later(j, _):
            sends(j, levels)
            return 0

        lax.fori_loop(1, PLANE, later, 0)

    everywhere = [(i, lax.rem(z + i, PLANES)) for i in range(PLANES)]

    def send_group(g):
        own(g).start()

        def copy(i, to, device):
            return pltpu.make_async_remote_copy(
                src_ref=packed.at[g, to],
                dst_ref=landed.at[g - 1, stn, tim],
                send_sem=send_sem.at[g - 1],
                recv_sem=recv_sem.at[g - 1],
                device_id=device,
                device_id_type=MESH,
            )

        send_planes(copy, everywhere)

    def some(ref, count):
        return ref.at[0, pl.ds(0, count)]

    def wait_for(sem, count):
        tiles = some(packed, count)
        pltpu.make_async_copy(tiles, tiles, sem).wait()

    def ours(i):
        return (z + PLANES + side * i) % PLANES

    def theirs(i):
        return (z + PLANES - side * (1 + i)) % PLANES

    def tell(slot_from, step, to):
        for i in range(SIDE):
            pltpu.make_async_remote_copy(
                src_ref=packed.at[slot_from, pl.ds(theirs(i) * PLANE, PLANE)],
                dst_ref=heard.at[step, pl.ds(i * PLANE, PLANE)],
                send_sem=heard_send.at[step],
                recv_sem=heard_recv.at[step],
                device_id=(stn, to),
                device_id_type=MESH,
            ).start()

    def join(slot_from, step):
        def add(n, _):
            at = pl.multiple_of(ours(n // 4) * PLANE + (n % 4) * 8, 8)
            here = packed[slot_from, pl.ds(at, 8)].astype(F32)
            there = heard[step, pl.ds(n * 8, 8)].astype(F32)
            joined[step, pl.ds(n * 8, 8)] = (here + there).astype(BF16)
            return 0

        lax.fori_loop(0, SIDE * PLANE // 8, add, 0)

    def send_border(step, piece, sem):
        def copy(i, to, device):
            return pltpu.make_async_remote_copy(
                src_ref=joined.at[step, i * PLANE + lax.rem(to, PLANE)],
                dst_ref=border_out.at[stn, piece],
                send_sem=sem,
                recv_sem=recv_sem.at[GROUPS - 1],
                device_id=device,
                device_id_type=MESH,
            )

        send_planes(copy, [(i, ours(i)) for i in range(SIDE)])

    filter_group(x, w, stage, TE, 0, -TAPS, TE, TE)
    greet_pass(ready, stations, pieces)
    finish(1)
    pl.semaphore_wait(ready, pieces - 1)
    send_group(1)
    copies[1].wait()
    filter_group(x, w, stage, T - TAPS + 1, TAPS - 1, 0, TAPS - 1, TE - 1)
    finish(front)

    @pl.when(tim < pieces - 1)
    def _():
        tell(front, 0, tim + 1)

    filter_group(x, w, stage, 0, 0, 0, TE, TE)
    finish(back)

    @pl.when(tim > 0)
    def _():
        tell(back, 1, tim - 1)

    for g in (2, 3):
        filter_group(x, w, stage, g * TE, 0, -TAPS, TE, TE)
        finish(g)
        send_group(g)

    @pl.when(tim > 0)
    def _():
        wait_for(heard_recv.at[0], SIDE * PLANE)
        join(back, 0)
        pltpu.make_async_copy(
            joined.at[0, w_me], border_out.at[stn, tim], own_sem.at[GROUPS - 1]
        ).start()
        send_border(0, tim, border_send.at[0])

    @pl.when(tim == 0)
    def _():
        pltpu.make_async_copy(
            packed.at[back, me], border_out.at[stn, tim], own_sem.at[GROUPS - 1]
        ).start()

        def copy(i, to, device):
            return pltpu.make_async_remote_copy(
                src_ref=packed.at[back, to],
                dst_ref=border_out.at[stn, tim],
                send_sem=border_send.at[0],
                recv_sem=recv_sem.at[GROUPS - 1],
                device_id=device,
                device_id_type=MESH,
            )

        send_planes(copy, everywhere)

    @pl.when(tim < pieces - 1)
    def _():
        wait_for(heard_recv.at[1], SIDE * PLANE)
        join(front, 1)
        pltpu.make_async_copy(
            joined.at[1, w_me], border_out.at[stn, tim + 1], own_sem.at[GROUPS]
        ).start()
        send_border(1, tim + 1, border_send.at[1])

    for g in range(1, GROUPS):
        own(g).wait()
        wait_for(recv_sem.at[g - 1], devices - 1)
        for r in range(RADIX):

            def collect(n, _, g=g, r=r):
                gather(landed.at[g - 1], values, crossed, r, n * 8, 8)
                return 0

            lax.fori_loop(0, stations // 8, collect, 0)

            def multiply(i, _, g=g, r=r):
                rows = pl.ds(pl.multiple_of(i * 256, 256), 256)
                for q, other in enumerate((values, crossed)):
                    more = dft(values[r, rows, :], other[r])
                    if g > 1:
                        more = power[r, q, rows, :] + more
                    power[r, q, rows, :] = more
                return 0

            lax.fori_loop(0, inputs // 256, multiply, 0)
            if g == GROUPS - 1:
                pltpu.make_async_copy(power.at[r], power_out.at[r], load_sem.at[0]).start()
                pltpu.make_async_copy(power.at[r], power_out.at[r], load_sem.at[0]).wait()

    for g in range(1, GROUPS):
        wait_for(send_sem.at[g - 1], devices - 1)

    def own_border(i):
        pltpu.make_async_copy(packed.at[0, 0], packed.at[0, 1], own_sem.at[i]).wait()

    own_border(GROUPS - 1)

    @pl.when(tim == 0)
    def _():
        wait_for(border_send.at[0], devices - 1)

    @pl.when(tim > 0)
    def _():
        wait_for(heard_send.at[1], SIDE * PLANE)
        wait_for(border_send.at[0], SIDE * PLANE - 1)

    @pl.when(tim < pieces - 1)
    def _():
        wait_for(heard_send.at[0], SIDE * PLANE)
        wait_for(border_send.at[1], SIDE * PLANE - 1)
        own_border(GROUPS)
        wait_for(recv_sem.at[GROUPS - 1], devices - 2)

    @pl.when(tim == pieces - 1)
    def _():
        wait_for(recv_sem.at[GROUPS - 1], devices - 1)


def last_kernel(power, tiles, out, values, crossed):
    step = pl.program_id(0)
    pieces = tiles.shape[1]
    for r in range(RADIX):

        @pl.when(step == r)
        def _(r=r):
            gather(tiles, values, crossed, r, 0, tiles.shape[0])

            for q, other in enumerate((values, crossed)):
                more = dft(values[r], other[r])
                out[0, q] = (power[0, q] + more) * (1.0 / (pieces * T))


def per_device(voltages, taps_weight):
    stations, pieces = lax.axis_size("stn"), lax.axis_size("tim")
    devices = stations * pieces
    inputs = stations * A
    any_space = pl.BlockSpec(memory_space=pl.ANY)
    vmem = pl.BlockSpec(memory_space=pltpu.VMEM)
    lanes = pieces * 2 * TE
    operands = (voltages, taps_weight, jnp.asarray(tables()))
    power, border = pl.pallas_call(
        lambda *refs: front_kernel(stations, pieces, *refs),
        out_shape=[
            jax.ShapeDtypeStruct((RADIX, 2, inputs, inputs), F32),
            jax.ShapeDtypeStruct((stations, pieces, A, LANES), BF16),
        ],
        in_specs=[any_space, vmem, vmem],
        out_specs=[any_space] * 2,
        scratch_shapes=[
            pltpu.VMEM((2, A, T * K), BF16),
            pltpu.VMEM((2 * CHUNKS * A * TE, LANES), F32),
            pltpu.VMEM((RADIX, A * 2 * TE, 2 * QUARTER), BF16),
            pltpu.VMEM((RADIX, QUARTER, A * 2 * TE), F32),
            pltpu.VMEM((QUARTER * A, LANES), F32),
            pltpu.VMEM((GROUPS + 1, devices, A, LANES), BF16),
            pltpu.VMEM((2, SIDE * PLANE, A, LANES), BF16),
            pltpu.VMEM((2, SIDE * PLANE, A, LANES), BF16),
            pltpu.VMEM((GROUPS - 1, stations, pieces, A, LANES), BF16),
            pltpu.VMEM((RADIX, inputs, lanes), BF16),
            pltpu.VMEM((RADIX, inputs, lanes), BF16),
            pltpu.VMEM((RADIX, 2, inputs, inputs), F32),
            pltpu.SemaphoreType.REGULAR,
            pltpu.SemaphoreType.DMA((2,)),
            pltpu.SemaphoreType.DMA((GROUPS + 1,)),
            pltpu.SemaphoreType.DMA((GROUPS - 1,)),
            pltpu.SemaphoreType.DMA((GROUPS,)),
            pltpu.SemaphoreType.DMA((2,)),
            pltpu.SemaphoreType.DMA((2,)),
            pltpu.SemaphoreType.DMA((2,)),
        ],
        compiler_params=pltpu.CompilerParams(
            collective_id=0, has_side_effects=True, vmem_limit_bytes=36 << 20
        ),
    )(*(pltpu.with_memory_space_constraint(v, pltpu.HBM) for v in operands))
    block = pl.BlockSpec((1, 2, inputs, inputs), lambda r: (r, 0, 0, 0))
    return pl.pallas_call(
        last_kernel,
        grid=(RADIX,),
        out_shape=jax.ShapeDtypeStruct((RADIX, 2, inputs, inputs), F32),
        in_specs=[
            block,
            pl.BlockSpec((stations, pieces, A, LANES), lambda r: (0, 0, 0, 0)),
        ],
        out_specs=block,
        scratch_shapes=[
            pltpu.VMEM((RADIX, inputs, lanes), BF16),
            pltpu.VMEM((RADIX, inputs, lanes), BF16),
        ],
        compiler_params=pltpu.CompilerParams(vmem_limit_bytes=24 << 20),
    )(power, border)


def solution(mesh):
    return jax.shard_map(
        per_device,
        mesh=mesh,
        in_specs=(P(None, "stn", "tim"), P()),
        out_specs=P(("stn", "tim"), None, None, None),
        check_vma=False,
    )
```

```python
import math

import jax
import jax.numpy as jnp
import ml_dtypes
import numpy as np
from jax import lax
from jax.experimental import pallas as pl
from jax.experimental.pallas import tpu as pltpu
from jax.sharding import PartitionSpec as P

K = 1024
TAPS = 16
RADIX = 4
QUARTER = K // RADIX
LANES = 128
CHUNKS = K // LANES
A = 16
T = 64
TE = 16
GROUPS = T // TE
PLANES = 8
PLANE = 32
SIDE = PLANES // 2
MESH = pl.DeviceIdType.MESH
F32, BF16 = jnp.float32, jnp.bfloat16


def place(u, pieces):
    z, w = u // PLANE, u % PLANE
    return (z // 2) * 8 + w // 4, (w % 4) * 2 + z % 2


def tables():
    stn, tim = place(np.arange(QUARTER), 8)
    k = (stn * 8 + tim)[None, :, None] * RADIX + np.arange(RADIX)[:, None, None]
    phase = (k * np.arange(QUARTER)[None, None, :]) % K
    angle = phase.astype(np.float64) * (2.0 * math.pi / K)
    both = np.concatenate([np.cos(angle), np.sin(angle)], axis=2)
    return both.astype(np.float32).astype(ml_dtypes.bfloat16)


def greet_start(stations, pieces):
    stn, tim = lax.axis_index("stn"), lax.axis_index("tim")
    barrier = pltpu.get_barrier_semaphore()

    def column(i, _):
        pl.semaphore_signal(
            barrier, inc=1, device_id=((stn + i) % stations, tim), device_id_type=MESH
        )
        return 0

    lax.fori_loop(1, stations, column, 0)

    def row(i, _):
        pl.semaphore_signal(
            barrier, inc=1, device_id=(stn, (tim + i) % pieces), device_id_type=MESH
        )
        return 0

    lax.fori_loop(1, pieces, row, 0)


def greet_pass(ready, stations, pieces):
    stn, tim = lax.axis_index("stn"), lax.axis_index("tim")
    pl.semaphore_wait(pltpu.get_barrier_semaphore(), stations + pieces - 2)

    def passed(i, _):
        pl.semaphore_signal(
            ready, inc=1, device_id=(stn, (tim + i) % pieces), device_id_type=MESH
        )
        return 0

    lax.fori_loop(1, pieces, passed, 0)


def fir_outputs(load, weights, times, low, high):
    blocks = {}
    outs = []
    for t in times:
        total = None
        for p in range(TAPS):
            b = t - p
            if b < low or b >= high:
                continue
            if b not in blocks:
                blocks[b] = load(b)
            term = weights[p] * blocks[b]
            total = term if total is None else total + term
        outs.append(total)
    return outs


def filter_group(x, w, stage, first, start_time, low, high, count):
    def one(i, _):
        q, c = i // CHUNKS, i % CHUNKS
        lanes = pl.multiple_of(c * LANES, LANES)
        weights = [
            jnp.broadcast_to(w[pl.ds(p, 1), pl.ds(lanes, LANES)], (A, LANES))
            for p in range(TAPS)
        ]

        def load(b):
            at = pl.multiple_of((first + b) * K + lanes, LANES)
            return x[q, :, pl.ds(at, LANES)].astype(F32)

        outs = fir_outputs(load, weights, range(start_time, start_time + count), low, high)
        base = i * A * TE
        for t, out in enumerate(outs):
            stage[pl.ds(base + t, A, stride=TE), :] = out
        if count < TE:
            stage[pl.ds(base + count, A, stride=TE), :] = jnp.zeros((A, LANES), F32)
        return 0

    lax.fori_loop(0, 2 * CHUNKS, one, 0)


def butterfly(stage, rows, h, length):
    v = []
    for q in range(2):
        for j in range(RADIX):
            base = (q * CHUNKS + 2 * j + h) * A * length
            v.append(stage[pl.ds(base + rows, length), :])
    re, im = v[:4], v[4:]
    a0r, a0i = re[0] + re[2], im[0] + im[2]
    a1r, a1i = re[0] - re[2], im[0] - im[2]
    b0r, b0i = re[1] + re[3], im[1] + im[3]
    b1r, b1i = re[1] - re[3], im[1] - im[3]
    return [
        (a0r + b0r, a0i + b0i),
        (a1r + b1i, a1i - b1r),
        (a0r - b0r, a0i - b0i),
        (a1r - b1i, a1i + b1r),
    ]


def dft(table, rows):
    return lax.dot_general(
        table, rows, (((1,), (1,)), ((), ())), preferred_element_type=F32
    )


def transform_group(table, stage, mixed, halves, turned, packed, slot_to):
    def mix(a, _):
        group = (a // 4) * 128 + (a % 4) * TE
        for h in range(2):
            for r, (re, im) in enumerate(butterfly(stage, a * TE, h, TE)):
                top = pl.ds(pl.multiple_of(group, TE), TE)
                low = pl.ds(pl.multiple_of(group + 64, TE), TE)
                near = pl.ds(h * LANES, LANES)
                far = pl.ds(QUARTER + h * LANES, LANES)
                mixed[r, top, near] = re.astype(BF16)
                mixed[r, top, far] = im.astype(BF16)
                mixed[r, low, near] = im.astype(BF16)
                mixed[r, low, far] = (-re).astype(BF16)
        return 0

    lax.fori_loop(0, A, mix, 0)
    slot = (lax.broadcasted_iota(jnp.int32, (QUARTER, LANES), 1) % 64) // TE
    for r in range(RADIX):
        halves[r] = dft(table[r], mixed[r])

    def turn(high, _):
        at = pl.multiple_of(high * LANES, LANES)
        parts = [halves[r, :, pl.ds(at, LANES)] for r in range(RADIX)]
        for low in range(4):
            turned[pl.ds(high * 4 + low, QUARTER, stride=A), :] = regroup(parts, low, slot)
        return 0

    lax.fori_loop(0, 4, turn, 0)

    def pack(i, _):
        rows = turned[pl.ds(pl.multiple_of(i * 512, 512), 512), :]
        packed[slot_to, pl.ds(pl.multiple_of(i * 32, 32), 32)] = rows.astype(BF16).reshape(
            32, A, LANES
        )
        return 0

    lax.fori_loop(0, QUARTER * A // 512, pack, 0)


def regroup(parts, low, slot):
    out = None
    for i, part in enumerate(parts):
        moved = part
        if i != low:
            moved = pltpu.roll(part, (TE * (i - low)) % LANES, 1)
        out = moved if out is None else jnp.where(slot == i, moved, out)
    return out


def gather(tiles, values, crossed, r, start, stations):
    rows = stations * A
    at = pl.ds(pl.multiple_of(start * A, A), rows)
    lane = lax.broadcasted_iota(jnp.int32, (rows, LANES), 1)
    slot = (lane % 64) // TE
    for half in range(2):
        parts = [
            tiles[pl.ds(start, stations), half * 4 + i].reshape(rows, LANES).astype(F32)
            for i in range(4)
        ]
        out = regroup(parts, r, slot)
        other = pltpu.roll(out, 64, 1)
        lanes = pl.ds(half * LANES, LANES)
        values[r, at, lanes] = out.astype(BF16)
        crossed[r, at, lanes] = jnp.where(lane < 64, -other, other).astype(BF16)


def front_kernel(
    stations,
    pieces,
    x_hbm,
    w,
    table_hbm,
    power_out,
    last_out,
    table,
    x,
    stage,
    mixed,
    halves,
    turned,
    packed,
    heard,
    joined,
    landed,
    values,
    crossed,
    power,
    ready,
    load_sem,
    own_sem,
    send_sem,
    recv_sem,
    heard_send,
    heard_recv,
    border_send,
):
    devices = stations * pieces
    inputs = stations * A
    stn, tim = lax.axis_index("stn"), lax.axis_index("tim")
    z, w_me = (stn // 8) * 2 + tim % 2, (stn % 8) * 4 + tim // 2
    me = z * PLANE + w_me
    side = 2 * (z % 2) - 1
    front, back = GROUPS, 0
    copies = []
    for i in range(2):
        part = pl.ds(i * (T // 2) * K, (T // 2) * K)
        copy = pltpu.make_async_copy(x_hbm.at[:, :, part], x.at[:, :, part], load_sem.at[i])
        copy.start()
        copies.append(copy)
    fetch = pltpu.make_async_copy(table_hbm, table, load_sem.at[2])
    fetch.start()
    greet_start(stations, pieces)
    copies[0].wait()

    def finish(slot_to):
        transform_group(table, stage, mixed, halves, turned, packed, slot_to)

    def landing(g):
        return last_out if g == GROUPS - 1 else landed.at[g - 1]

    def own(g):
        return pltpu.make_async_copy(
            packed.at[g, me], landing(g).at[stn, tim], own_sem.at[g - 1]
        )

    def send_planes(copy, planes):
        levels = [(i, p * PLANE, lax.div(p, 2) * 8, lax.rem(p, 2)) for i, p in planes]

        def sends(j, levels):
            to = lax.rem(w_me + j * 13, PLANE)
            row, column = lax.div(to, 4), lax.rem(to, 4) * 2
            for i, start, stn_base, tim_base in levels:
                copy(i, start + to, (stn_base + row, tim_base + column)).start()

        sends(0, levels[1:])

        def later(j, _):
            sends(j, levels)
            return 0

        lax.fori_loop(1, PLANE, later, 0)

    everywhere = [(i, lax.rem(z + i, PLANES)) for i in range(PLANES)]

    def send_group(g):
        own(g).start()

        def copy(i, to, device):
            return pltpu.make_async_remote_copy(
                src_ref=packed.at[g, to],
                dst_ref=landing(g).at[stn, tim],
                send_sem=send_sem.at[g - 1],
                recv_sem=recv_sem.at[g - 1],
                device_id=device,
                device_id_type=MESH,
            )

        send_planes(copy, everywhere)

    def some(ref, count):
        return ref.at[0, pl.ds(0, count)]

    def wait_for(sem, count):
        tiles = some(packed, count)
        pltpu.make_async_copy(tiles, tiles, sem).wait()

    def ours(i):
        return (z + PLANES + side * i) % PLANES

    def theirs(i):
        return (z + PLANES - side * (1 + i)) % PLANES

    def tell(slot_from, step, to):
        for i in range(SIDE):
            pltpu.make_async_remote_copy(
                src_ref=packed.at[slot_from, pl.ds(theirs(i) * PLANE, PLANE)],
                dst_ref=heard.at[step, pl.ds(i * PLANE, PLANE)],
                send_sem=heard_send.at[step],
                recv_sem=heard_recv.at[step],
                device_id=(stn, to),
                device_id_type=MESH,
            ).start()

    def join(slot_from, step):
        def add(n, _):
            at = pl.multiple_of(ours(n // 4) * PLANE + (n % 4) * 8, 8)
            here = packed[slot_from, pl.ds(at, 8)].astype(F32)
            there = heard[step, pl.ds(n * 8, 8)].astype(F32)
            joined[step, pl.ds(n * 8, 8)] = (here + there).astype(BF16)
            return 0

        lax.fori_loop(0, SIDE * PLANE // 8, add, 0)

    def send_border(step, piece, sem):
        def copy(i, to, device):
            return pltpu.make_async_remote_copy(
                src_ref=joined.at[step, i * PLANE + lax.rem(to, PLANE)],
                dst_ref=landed.at[GROUPS - 2, stn, piece],
                send_sem=sem,
                recv_sem=recv_sem.at[GROUPS - 1],
                device_id=device,
                device_id_type=MESH,
            )

        send_planes(copy, [(i, ours(i)) for i in range(SIDE)])

    filter_group(x, w, stage, TE, 0, -TAPS, TE, TE)
    greet_pass(ready, stations, pieces)
    fetch.wait()
    finish(1)
    pl.semaphore_wait(ready, pieces - 1)
    send_group(1)
    copies[1].wait()
    filter_group(x, w, stage, T - TAPS + 1, TAPS - 1, 0, TAPS - 1, TE - 1)
    finish(front)

    @pl.when(tim < pieces - 1)
    def _():
        tell(front, 0, tim + 1)

    filter_group(x, w, stage, 0, 0, 0, TE, TE)
    finish(back)

    @pl.when(tim > 0)
    def _():
        tell(back, 1, tim - 1)

    for g in (2, 3):
        filter_group(x, w, stage, g * TE, 0, -TAPS, TE, TE)
        finish(g)
        if g == 2:
            send_group(g)

    @pl.when(tim > 0)
    def _():
        wait_for(heard_recv.at[0], SIDE * PLANE)
        join(back, 0)
        pltpu.make_async_copy(
            joined.at[0, w_me], landed.at[GROUPS - 2, stn, tim], own_sem.at[GROUPS - 1]
        ).start()
        send_border(0, tim, border_send.at[0])

    @pl.when(tim == 0)
    def _():
        pltpu.make_async_copy(
            packed.at[back, me], landed.at[GROUPS - 2, stn, tim], own_sem.at[GROUPS - 1]
        ).start()

        def copy(i, to, device):
            return pltpu.make_async_remote_copy(
                src_ref=packed.at[back, to],
                dst_ref=landed.at[GROUPS - 2, stn, tim],
                send_sem=border_send.at[0],
                recv_sem=recv_sem.at[GROUPS - 1],
                device_id=device,
                device_id_type=MESH,
            )

        send_planes(copy, everywhere)

    @pl.when(tim < pieces - 1)
    def _():
        wait_for(heard_recv.at[1], SIDE * PLANE)
        join(front, 1)
        pltpu.make_async_copy(
            joined.at[1, w_me], landed.at[GROUPS - 2, stn, tim + 1], own_sem.at[GROUPS]
        ).start()
        send_border(1, tim + 1, border_send.at[1])

    send_group(GROUPS - 1)

    def own_border(i):
        pltpu.make_async_copy(packed.at[0, 0], packed.at[0, 1], own_sem.at[i]).wait()

    for g in range(1, GROUPS):
        if g < GROUPS - 1:
            own(g).wait()
            wait_for(recv_sem.at[g - 1], devices - 1)
        else:
            own_border(GROUPS - 1)

            @pl.when(tim < pieces - 1)
            def _():
                own_border(GROUPS)
                wait_for(recv_sem.at[GROUPS - 1], devices - 2)

            @pl.when(tim == pieces - 1)
            def _():
                wait_for(recv_sem.at[GROUPS - 1], devices - 1)

        for r in range(RADIX):

            def collect(n, _, g=g, r=r):
                gather(landed.at[g - 1], values, crossed, r, n * 8, 8)
                return 0

            lax.fori_loop(0, stations // 8, collect, 0)

            def multiply(i, _, g=g, r=r):
                rows = pl.ds(pl.multiple_of(i * 256, 256), 256)
                for q, other in enumerate((values, crossed)):
                    more = dft(values[r, rows, :], other[r])
                    if g > 1:
                        more = power[r, q, rows, :] + more
                    power[r, q, rows, :] = more
                return 0

            lax.fori_loop(0, inputs // 256, multiply, 0)
            if g == GROUPS - 1:
                pltpu.make_async_copy(power.at[r], power_out.at[r], load_sem.at[0]).start()
                pltpu.make_async_copy(power.at[r], power_out.at[r], load_sem.at[0]).wait()

    for g in range(1, GROUPS):
        wait_for(send_sem.at[g - 1], devices - 1)

    @pl.when(tim == 0)
    def _():
        wait_for(border_send.at[0], devices - 1)

    @pl.when(tim > 0)
    def _():
        wait_for(heard_send.at[1], SIDE * PLANE)
        wait_for(border_send.at[0], SIDE * PLANE - 1)

    @pl.when(tim < pieces - 1)
    def _():
        wait_for(heard_send.at[0], SIDE * PLANE)
        wait_for(border_send.at[1], SIDE * PLANE - 1)

    own(GROUPS - 1).wait()
    wait_for(recv_sem.at[GROUPS - 2], devices - 1)


def last_kernel(power, tiles, out, values, crossed):
    step = pl.program_id(0)
    pieces = tiles.shape[1]
    for r in range(RADIX):

        @pl.when(step == r)
        def _(r=r):
            gather(tiles, values, crossed, r, 0, tiles.shape[0])

            for q, other in enumerate((values, crossed)):
                more = dft(values[r], other[r])
                out[0, q] = (power[0, q] + more) * (1.0 / (pieces * T))


def per_device(voltages, taps_weight):
    stations, pieces = lax.axis_size("stn"), lax.axis_size("tim")
    devices = stations * pieces
    inputs = stations * A
    any_space = pl.BlockSpec(memory_space=pl.ANY)
    vmem = pl.BlockSpec(memory_space=pltpu.VMEM)
    lanes = pieces * 2 * TE
    operands = (voltages, taps_weight, jnp.asarray(tables()))
    power, last = pl.pallas_call(
        lambda *refs: front_kernel(stations, pieces, *refs),
        out_shape=[
            jax.ShapeDtypeStruct((RADIX, 2, inputs, inputs), F32),
            jax.ShapeDtypeStruct((stations, pieces, A, LANES), BF16),
        ],
        in_specs=[any_space, vmem, any_space],
        out_specs=[any_space] * 2,
        scratch_shapes=[
            pltpu.VMEM((RADIX, QUARTER, 2 * QUARTER), BF16),
            pltpu.VMEM((2, A, T * K), BF16),
            pltpu.VMEM((2 * CHUNKS * A * TE, LANES), F32),
            pltpu.VMEM((RADIX, A * 2 * TE, 2 * QUARTER), BF16),
            pltpu.VMEM((RADIX, QUARTER, A * 2 * TE), F32),
            pltpu.VMEM((QUARTER * A, LANES), F32),
            pltpu.VMEM((GROUPS + 1, devices, A, LANES), BF16),
            pltpu.VMEM((2, SIDE * PLANE, A, LANES), BF16),
            pltpu.VMEM((2, SIDE * PLANE, A, LANES), BF16),
            pltpu.VMEM((GROUPS - 1, stations, pieces, A, LANES), BF16),
            pltpu.VMEM((RADIX, inputs, lanes), BF16),
            pltpu.VMEM((RADIX, inputs, lanes), BF16),
            pltpu.VMEM((RADIX, 2, inputs, inputs), F32),
            pltpu.SemaphoreType.REGULAR,
            pltpu.SemaphoreType.DMA((3,)),
            pltpu.SemaphoreType.DMA((GROUPS + 1,)),
            pltpu.SemaphoreType.DMA((GROUPS - 1,)),
            pltpu.SemaphoreType.DMA((GROUPS,)),
            pltpu.SemaphoreType.DMA((2,)),
            pltpu.SemaphoreType.DMA((2,)),
            pltpu.SemaphoreType.DMA((2,)),
        ],
        compiler_params=pltpu.CompilerParams(
            collective_id=0, has_side_effects=True, vmem_limit_bytes=36 << 20
        ),
    )(*(pltpu.with_memory_space_constraint(v, pltpu.HBM) for v in operands))
    block = pl.BlockSpec((1, 2, inputs, inputs), lambda r: (r, 0, 0, 0))
    return pl.pallas_call(
        last_kernel,
        grid=(RADIX,),
        out_shape=jax.ShapeDtypeStruct((RADIX, 2, inputs, inputs), F32),
        in_specs=[
            block,
            pl.BlockSpec((stations, pieces, A, LANES), lambda r: (0, 0, 0, 0)),
        ],
        out_specs=block,
        scratch_shapes=[
            pltpu.VMEM((RADIX, inputs, lanes), BF16),
            pltpu.VMEM((RADIX, inputs, lanes), BF16),
        ],
        compiler_params=pltpu.CompilerParams(vmem_limit_bytes=24 << 20),
    )(power, last)


def solution(mesh):
    return jax.shard_map(
        per_device,
        mesh=mesh,
        in_specs=(P(None, "stn", "tim"), P()),
        out_specs=P(("stn", "tim"), None, None, None),
        check_vma=False,
    )
```
